1024 devices in a mesh: gr: 128 (over z_lo, y, core), gc: 8 (over x, z_hi).
Axes of the slice: x: 4, y: 4, z: 32 (z_hi: 2, z_lo: 16; z = z_hi * 16 + z_lo), core: 2. Of those that a mesh axis runs over, the one named last changes fastest.
Arguments:
- density: float32 [1024, 9, 128, 128], P(('gr', 'gc')), as said below
- reach: int32 [1024], replicated, may hold values from 1 to 4, as said below
Outputs:
- purified: float32 [1024, 9, 128, 128], P(('gr', 'gc'))
The draws below stay inside these ranges and needn't reach their ends.
Inputs may be any that keep to these rules, and one draw needn't show every extreme that they name: Every 16th block row, from row 0, has reach 4. `density`: Symmetric: block (i, i + d) is the transpose of block (i + d, i); blocks outside the pattern given by reach are zero.
All inputs are finite; a program needn't handle non-finite values.
Results may differ from the reference program's by a relative error of at most 0.022.
Values sent between devices are 32-bit elements; how exact they have to be, the bound alone decides.
A program may use at most 64 MiB of HBM per device.

```python
import jax
import jax.numpy as jnp
from jax import lax

BS = 128
HALF = 4
STEPS = 2
NB = 1024


def pattern_reach(key):
    inner_key = jax.random.fold_in(key, 11)
    drawn = jax.random.randint(inner_key, (NB,), 1, HALF + 1).astype(jnp.int32)
    places = jnp.arange(NB, dtype=jnp.int32)
    return jnp.where(places % 16 == 0, HALF, drawn).astype(jnp.int32)


def draw_reach(key, part):
    return pattern_reach(key)


def draw_density(key, part):
    reach = pattern_reach(key)
    key = jax.random.fold_in(key, 5)
    width = 2 * HALF + 1
    offsets = jnp.arange(-HALF, HALF + 1, dtype=jnp.int32)
    places = jnp.arange(NB, dtype=jnp.int32)
    nearby = reach[(places[:, None] + offsets[None, :]) % NB]
    keep = (jnp.abs(offsets)[None, :] <= jnp.minimum(reach[:, None], nearby)).astype(jnp.float32)
    spread = 0.35 / (BS * width) ** 0.5
    raw = jax.random.normal(key, (NB, width, BS, BS), jnp.float32)
    raw = raw * spread
    blocks = []
    for column in range(width):
        offset = column - HALF
        partner = jnp.roll(raw[:, width - 1 - column], -offset, axis=0)
        blocks.append(0.5 * (raw[:, column] + jnp.swapaxes(partner, 1, 2)))
    sym = jnp.stack(blocks, axis=1)
    eye_block = 0.5 * jnp.eye(BS, dtype=jnp.float32)
    sym = sym.at[:, HALF].add(eye_block[None])
    return sym * keep[:, :, None, None]


def setup_inputs(seed: int = 0) -> dict:
    key_of = jax.random.split(jax.random.key(seed), 3)
    return {
        "density": draw_density(jax.random.fold_in(key_of[2], 71), 0),
        "reach": draw_reach(jax.random.fold_in(key_of[2], 71), 0),
    }


def pattern(reach):
    total = reach.shape[0]
    offsets = jnp.arange(-HALF, HALF + 1, dtype=jnp.int32)
    rows_all = jnp.arange(total, dtype=jnp.int32)
    nearby = reach[(rows_all[:, None] + offsets[None, :]) % total]
    limit = jnp.minimum(reach[:, None], nearby)
    return (jnp.abs(offsets)[None, :] <= limit).astype(jnp.float32)


def product(left, right, keep):
    blocks = []
    for target in range(-HALF, HALF + 1):
        summed = jnp.zeros(left[:, 0].shape, jnp.float32)
        for inner in range(max(-HALF, target - HALF), min(HALF, target + HALF) + 1):
            shifted = jnp.roll(right[:, target - inner + HALF], -inner, axis=0)
            summed = summed + jnp.einsum("nab,nbc->nac", left[:, inner + HALF], shifted,
                                         precision=lax.Precision.HIGHEST)
        blocks.append(summed)
    return jnp.stack(blocks, axis=1) * keep[:, :, None, None]


def reference(density, reach):
    keep = pattern(reach)
    current = density
    for sweep in range(STEPS):
        square = product(current, current, keep)
        cube = product(square, current, keep)
        current = 3.0 * square - 2.0 * cube
    return current
```

```python
import jax
import jax.numpy as jnp
from jax import lax
from jax.experimental import pallas as pl
from jax.experimental.pallas import tpu as pltpu
from jax.sharding import PartitionSpec as P

MESH = pl.DeviceIdType.MESH
BS = 128
G = 2 * BS
F32 = jnp.float32
BF16 = jnp.bfloat16
NT = (((1,), (1,)), ((), ()))
NN = (((1,), (0,)), ((), ()))


def exchange(lines, x_ref, own, par, ssem, rsem, lsem):
    gr, gc = lax.axis_index("gr"), lax.axis_index("gc")
    x, s = gc // 2, lax.rem(gc, 2)
    sg = 1 - 2 * s
    up = (lax.rem(gr + 1, lines), gc)
    down = (lax.rem(gr + lines - 1, lines), gc)
    partner_gc = gc + sg
    partner = (gr, partner_gc)
    across_up = (up[0], partner_gc)
    across_down = (down[0], partner_gc)
    last, first = gr == lines - 1, gr == 0
    others = [lax.rem(x + step, 4) for step in (1, 3, 2)]
    peers = [(gr, o * 2 + s) for o in others]

    barrier = pltpu.get_barrier_semaphore()
    for d in [partner, up, down] + peers:
        pl.semaphore_signal(barrier, inc=1, device_id=d, device_id_type=MESH)

    @pl.when(last)
    def _():
        pl.semaphore_signal(barrier, inc=1, device_id=across_up, device_id_type=MESH)

    @pl.when(first)
    def _():
        pl.semaphore_signal(barrier, inc=1, device_id=across_down, device_id_type=MESH)

    extra = jnp.where(last, 1, 0) + jnp.where(first, 1, 0)
    pl.semaphore_wait(barrier, 6 + extra)

    count = [0]
    pending = []

    def copy(src, dst, device, k=None):
        if k is None:
            k = count[0]
            count[0] += 1
        return pltpu.make_async_remote_copy(src, dst, ssem.at[k], rsem.at[k], device_id=device, device_id_type=MESH)

    def send(src, dst, device):
        c = copy(src, dst, device)
        c.start()
        pending.append(c)
        return c

    wide = pl.ds(3 - 3 * s, 6)
    far = 4 - 3 * sg
    w6 = pl.ds(0, 6)
    slot_up, slot_down = 4 - 4 * sg, 4 + 4 * sg

    cross = [send(x_ref.at[0, 4 - 2 * n * sg], par.at[4, n], partner) for n in range(3)]
    edge_up, edge_down = [], []
    for n in range(3):
        k_up, k_down = count[0], count[0] + 1
        count[0] += 2
        edge_up.append(k_up)
        edge_down.append(k_down)

        @pl.when(last)
        def _():
            copy(x_ref.at[0, 4 - 2 * n * sg], par.at[4 + 4 * sg, n], across_up, k_up).start()

        @pl.when(first)
        def _():
            copy(x_ref.at[0, 4 - 2 * n * sg], par.at[4 - 4 * sg, n], across_down, k_down).start()

    local = [
        pltpu.make_async_copy(x_ref.at[0, wide], own.at[4, w6], lsem.at[0]),
        pltpu.make_async_copy(x_ref.at[0, far], own.at[4, 6], lsem.at[1]),
    ]
    for c in local:
        c.start()
    near = []
    for dst, slot in ((up, slot_up), (down, slot_down)):
        near.append(send(x_ref.at[0, wide], own.at[slot, w6], dst))
        near.append(send(x_ref.at[0, far], own.at[slot, 6], dst))
    arrive = []
    for o, dst in zip(others, peers):
        slot = 4 + sg * (x - o)
        arrive.append(send(x_ref.at[0, wide], own.at[slot, w6], dst))
        arrive.append(send(x_ref.at[0, far], own.at[slot, 6], dst))
    for c in near:
        c.wait_recv()
    passed = []
    for o, dst in zip(others, peers):
        lower = o < x
        mine = jnp.where(lower, slot_up, slot_down)
        slot = 4 + sg * (x - o + jnp.where(lower, -4, 4))
        passed.append((mine, slot, dst))
        arrive.append(send(own.at[mine], own.at[slot], dst))
    for n in range(3):
        cross[n].wait_recv()
        c_up = copy(par.at[4, n], par.at[slot_up, n], up, edge_up[n])
        c_down = copy(par.at[4, n], par.at[slot_down, n], down, edge_down[n])

        @pl.when(jnp.logical_not(last))
        def _():
            c_up.start()

        @pl.when(jnp.logical_not(first))
        def _():
            c_down.start()

        pending.extend([c_up, c_down])
        for o, dst in zip(others, peers):
            arrive.append(send(par.at[4, n], par.at[4 + sg * (x - o), n], dst))
        c_up.wait_recv()
        c_down.wait_recv()
        for mine, slot, dst in passed:
            arrive.append(send(par.at[mine, n], par.at[slot, n], dst))
    for c in local:
        c.wait()
    for c in arrive:
        c.wait_recv()
    for c in pending:
        c.wait_send()


COPIES = 3 + 6 + 4 + 6 + 3 + 3 * 6


def split(v):
    hi = v.astype(BF16)
    return hi, (v - hi.astype(F32)).astype(BF16)


def dot3(ah, al, bh, bl, dims):
    def d(a, b):
        return lax.dot_general(a, b, dims, preferred_element_type=F32)

    return d(ah, bh) + d(ah, bl) + d(al, bh)


def evaluate(total, reach, own, par, out, xh, xl, sh, sl, nh, nl, rh, rl):
    gr, gc = lax.axis_index("gr"), lax.axis_index("gc")
    s = lax.rem(gc, 2)
    sg = 1 - 2 * s
    row = gr * 8 + gc
    at0 = 1 + 3 * s
    r = [reach[lax.rem(row + sg * (a - 8) + total, total)] for a in range(18)]

    def keep(a, b):
        ok = abs(a - b) <= jnp.minimum(r[a], r[b])
        return jnp.where(ok, 1.0, 0.0).astype(F32)

    def put(a, b, v):
        J, K = a // 2, b // 2
        rows = pl.ds((a % 2) * BS, BS)
        cols = pl.ds((K - J + 2) * G + (b % 2) * BS, BS)
        hi, lo = split(v)
        xh[J, rows, cols] = hi
        xl[J, rows, cols] = lo

    def both(a, b, v):
        if 0 <= b < 18:
            put(a, b, v)
            if a != b:
                put(b, a, v.T)

    zero = jnp.zeros((BS, BS), F32)
    for k in range(9):
        a = 2 * k
        for d in range(-1, 5):
            if d == -1 and k == 0:
                continue
            both(a, a + d, own[k, at0 + sg * d])
        both(a, a - 3, own[k, 6])
        for n in range(3):
            both(a + 1, a + 1 + 2 * n, par[k, n])
        if a + 5 < 18:
            put(a, a + 5, zero)
            put(a + 5, a, zero)

    def span(J, lo, hi):
        return pl.ds((lo - J + 2) * G, (hi - lo + 1) * G)

    def masked(J, K, v):
        return jnp.concatenate(
            [
                jnp.concatenate([v[:BS, :BS] * keep(2 * J, 2 * K), v[:BS, BS:] * keep(2 * J, 2 * K + 1)], axis=1),
                jnp.concatenate([v[BS:, :BS] * keep(2 * J + 1, 2 * K), v[BS:, BS:] * keep(2 * J + 1, 2 * K + 1)], axis=1),
            ],
            axis=0,
        )

    for J in range(2, 7):
        for K in range(J - 2, J + 3):
            lo, hi = max(J, K) - 2, min(J, K) + 2
            a, b = span(J, lo, hi), span(K, lo, hi)
            v = masked(J, K, dot3(xh[J, :, a], xl[J, :, a], xh[K, :, b], xl[K, :, b], NT))
            cols = span(J, K, K)
            sh[J - 2, :, cols], sl[J - 2, :, cols] = split(v)
    for J in range(2, 7):
        for K in range(max(2, J - 2), min(6, J + 2) + 1):
            lo, hi = max(J, K) - 2, min(J, K) + 2
            a, b = span(J, lo, hi), span(K, lo, hi)
            cube = dot3(sh[J - 2, :, a], sl[J - 2, :, a], xh[K, :, b], xl[K, :, b], NT)
            cols = span(J, K, K)
            square = sh[J - 2, :, cols].astype(F32) + sl[J - 2, :, cols].astype(F32)
            hi_, lo_ = split(masked(J, K, 3.0 * square - 2.0 * cube))
            rows = span(K, J, J)
            nh[K - 2, rows, :] = hi_
            nl[K - 2, rows, :] = lo_
            if J == 4:
                rh[:, cols] = hi_[:BS]
                rl[:, cols] = lo_[:BS]
    squares = []
    for K in range(2, 7):
        lo, hi = max(4, K) - 2, min(4, K) + 2
        a, b = span(4, lo, hi), span(K, lo, hi)
        v = dot3(rh[:, a], rl[:, a], nh[K - 2, b, :], nl[K - 2, b, :], NN)
        v = jnp.concatenate([v[:, :BS] * keep(8, 2 * K), v[:, BS:] * keep(8, 2 * K + 1)], axis=1)
        squares.append(v)
    sq = [split(v) for v in squares]
    for K in range(2, 7):
        lo, hi = max(4, K) - 2, min(4, K) + 2
        b = span(K, lo, hi)
        ah = jnp.concatenate([sq[L - 2][0] for L in range(lo, hi + 1)], axis=1)
        al = jnp.concatenate([sq[L - 2][1] for L in range(lo, hi + 1)], axis=1)
        v = 3.0 * squares[K - 2] - 2.0 * dot3(ah, al, nh[K - 2, b, :], nl[K - 2, b, :], NN)
        for h in range(2):
            m = 2 * K + h
            if abs(m - 8) <= 4:
                out[0, 4 + sg * (m - 8)] = v[:, h * BS : (h + 1) * BS] * keep(8, m)


WORK = [
    pltpu.VMEM((9, G, 5 * G), BF16),
    pltpu.VMEM((9, G, 5 * G), BF16),
    pltpu.VMEM((5, G, 5 * G), BF16),
    pltpu.VMEM((5, G, 5 * G), BF16),
    pltpu.VMEM((5, 5 * G, G), BF16),
    pltpu.VMEM((5, 5 * G, G), BF16),
    pltpu.VMEM((BS, 5 * G), BF16),
    pltpu.VMEM((BS, 5 * G), BF16),
]
LAND = [(9, 7, BS, BS), (9, 3, BS, BS)]
SEMS = [pltpu.SemaphoreType.DMA((COPIES,)), pltpu.SemaphoreType.DMA((COPIES,)), pltpu.SemaphoreType.DMA((2,))]
VMEM_LIMIT = 58 << 20
MERGED = True


def solution(mesh):
    lines = mesh.shape["gr"]
    spec = P(("gr", "gc"), None, None, None)

    def local(density, reach):
        total = reach.shape[0]
        out = jax.ShapeDtypeStruct(density.shape, F32)
        smem = pl.BlockSpec(memory_space=pltpu.SMEM)
        vmem = pl.BlockSpec(memory_space=pltpu.VMEM)
        hbm = pl.BlockSpec(memory_space=pl.ANY)
        if MERGED:

            def kernel(reach_ref, x_ref, out_ref, own, par, ssem, rsem, lsem, *work):
                exchange(lines, x_ref, own, par, ssem, rsem, lsem)
                evaluate(total, reach_ref, own, par, out_ref, *work)

            return pl.pallas_call(
                kernel,
                out_shape=out,
                in_specs=[smem, hbm],
                out_specs=vmem,
                scratch_shapes=[pltpu.VMEM(sh, F32) for sh in LAND] + SEMS + WORK,
                compiler_params=pltpu.CompilerParams(collective_id=0, has_side_effects=True, vmem_limit_bytes=VMEM_LIMIT),
            )(reach, density)

        def comm(x_ref, own, par, ssem, rsem, lsem):
            exchange(lines, x_ref, own, par, ssem, rsem, lsem)

        def comp(reach_ref, own, par, out_ref, *work):
            evaluate(total, reach_ref, own, par, out_ref, *work)

        own, par = pl.pallas_call(
            comm,
            out_shape=[jax.ShapeDtypeStruct(sh, F32) for sh in LAND],
            in_specs=[hbm],
            out_specs=[hbm, hbm],
            scratch_shapes=SEMS,
            compiler_params=pltpu.CompilerParams(collective_id=0, has_side_effects=True),
        )(density)
        return pl.pallas_call(
            comp,
            out_shape=out,
            in_specs=[smem, vmem, vmem],
            out_specs=vmem,
            scratch_shapes=WORK,
            compiler_params=pltpu.CompilerParams(vmem_limit_bytes=VMEM_LIMIT),
        )(reach, own, par)

    return jax.shard_map(local, mesh=mesh, in_specs=(spec, P()), out_specs=spec, check_vma=False)
```

```python
import jax
import jax.numpy as jnp
from jax import lax
from jax.experimental import pallas as pl
from jax.experimental.pallas import tpu as pltpu
from jax.sharding import PartitionSpec as P

MESH = pl.DeviceIdType.MESH
BS = 128
G = 2 * BS
F32 = jnp.float32
BF16 = jnp.bfloat16
NT = (((1,), (1,)), ((), ()))
NN = (((1,), (0,)), ((), ()))


def exchange(lines, x_ref, own, par, ssem, rsem, lsem, meanwhile=lambda: None):
    gr, gc = lax.axis_index("gr"), lax.axis_index("gc")
    x, s = gc // 2, lax.rem(gc, 2)
    sg = 1 - 2 * s
    side = 2 * lax.rem(gr, 2) - 1
    partner_gc = gc + sg
    partner = (gr, partner_gc)
    next_line = lax.rem(gr + side + lines, lines)
    out = (next_line, gc)
    mate = (gr - side, gc)
    steps = (1, 3, 2)
    others = [lax.rem(x + step, 4) for step in steps]
    peers = [(gr, o * 2 + s) for o in others]

    own_wide = pltpu.make_async_copy(x_ref.at[0, pl.ds(3 - 3 * s, 6)], own.at[4, pl.ds(0, 6)], lsem.at[0])
    own_far = pltpu.make_async_copy(x_ref.at[0, 4 - 3 * sg], own.at[4, 6], lsem.at[1])
    own_wide.start()
    own_far.start()

    barrier = pltpu.get_barrier_semaphore()
    pair, pairs = gr * 4 + x, lines * 4
    around, extra = [], 0
    for k in HOPS:
        q = pair + k
        wraps = jnp.logical_or(q < 0, q >= pairs)
        q = lax.rem(q + pairs, pairs)
        same = (q // 4, lax.rem(q, 4) * 2 + s)
        flipped = (same[0], same[1] + sg)
        around.append((k, wraps, same, flipped))
        extra = extra + jnp.where(wraps, 1, 0)
    for d in [partner] + [a[2] for a in around]:
        pl.semaphore_signal(barrier, inc=1, device_id=d, device_id_type=MESH)
    for _, wraps, _, flipped in around:

        @pl.when(wraps)
        def _(flipped=flipped):
            pl.semaphore_signal(barrier, inc=1, device_id=flipped, device_id_type=MESH)

    own_wide.wait()
    own_far.wait()
    pl.semaphore_wait(barrier, 1 + len(HOPS) + extra)

    pending = []

    def copy(src, dst, device, k, arrives=None):
        c = pltpu.make_async_remote_copy(
            src, dst, ssem.at[k], rsem.at[k if arrives is None else arrives], device_id=device, device_id_type=MESH
        )
        pending.append(c)
        return c

    slot_out, slot_back = 4 + 4 * sg * side, 4 - 4 * sg * side

    def routes(buffer, base, pick):
        def at(slot):
            return pick(buffer, slot)

        here = at(4)
        near = [copy(here, at(slot_back), out, base), copy(here, at(slot_out), mate, base + 1)]
        line, onward = [], []
        for j, (step, o, dst) in enumerate(zip(steps, others, peers)):
            line.append(copy(here, at(4 + sg * (x - o)), dst, base + 2 + j, base + 2 + (1, 0, 2)[j]))
            to_peer = (o - x) * side > 0
            src = jnp.where(to_peer, slot_out, 4 + sg * (o - x))
            k = jnp.where(to_peer, x - o, o - x)
            dst_slot = 4 + sg * (k + 4 * side)
            device = (jnp.where(to_peer, dst[0], mate[0]), jnp.where(to_peer, dst[1], mate[1]))
            arrives = base + 5 + jnp.where(to_peer, (1, 0, 2)[j], j)
            onward.append((to_peer, copy(at(src), at(dst_slot), device, base + 5 + j, arrives)))
        return near, line, onward

    def arrived(j, base, piece):
        return pltpu.make_async_remote_copy(
            piece, piece, ssem.at[base + 5 + j], rsem.at[base + 5 + j], device_id=mate, device_id_type=MESH
        )

    def start_if(cond, c):
        @pl.when(cond)
        def _():
            c.start()

    early = [routes(own, 5 + 8 * e, lambda ref, slot, p=p: ref.at[slot, p]) for e, p in enumerate(PIECES)]
    base = 5 + 8 * len(PIECES)
    cross = [
        copy(x_ref.at[(0, 4 - 2 * q[0] * sg) + q[1:]], par.at[(4,) + q], partner, n) for n, q in enumerate(PARTS)
    ]
    hot = (next_line // 8) != (gr // 8)

    for near, _, _ in early:
        near[0].start()
    for c in cross:
        c.start()
    late = []
    for n, q in enumerate(PARTS):
        copies = []
        for j, (k, wraps, same, flipped) in enumerate(around):
            sem, there = base + 8 * n + j, base + 8 * n + (j ^ 1)
            c = copy(par.at[(4,) + q], par.at[(4 - sg * k,) + q], same, sem, there)
            copies.append((wraps, c))
            own_row = pltpu.make_async_remote_copy(
                x_ref.at[(0, 4 - 2 * q[0] * sg) + q[1:]],
                par.at[(4 + sg * k,) + q],
                ssem.at[sem],
                rsem.at[there],
                device_id=flipped,
                device_id_type=MESH,
            )
            start_if(wraps, own_row)
        late.append(copies)
    for _, line, _ in early:
        for c in line:
            c.start()
    for near, _, _ in early:
        near[1].start()

    def pass_out(route):
        near, _, onward = route
        near[0].wait_recv()
        for to_peer, c in onward:
            start_if(to_peer, c)

    def pass_mate(route):
        _, line, onward = route
        for j, (to_peer, c) in enumerate(onward):
            line[(1, 0, 2)[j]].wait_recv()
            start_if(jnp.logical_not(to_peer), c)

    def spread(n):
        cross[n].wait_recv()
        for wraps, c in late[n]:
            start_if(jnp.logical_not(wraps), c)

    for route in early:
        pass_mate(route)
    spread(0)

    @pl.when(jnp.logical_not(hot))
    def _():
        for route in early:
            pass_out(route)

    for n in range(1, len(PARTS)):
        spread(n)

    @pl.when(hot)
    def _():
        for route in early:
            pass_out(route)

    for e, p in enumerate(PIECES):
        early[e][0][1].wait_recv()
        for j in range(3):
            arrived(j, 5 + 8 * e, own.at[4, p]).wait_recv()
    meanwhile()
    for copies in late:
        for _, c in copies:
            c.wait_recv()
    for c in pending:
        c.wait_send()


HOPS = (4, -4, 3, -3, 2, -2, 1, -1)
PIECES = (pl.ds(0, 7),)
PARTS = ((0,), (1,), (2,))
COPIES = 5 + 8 * len(PIECES) + 8 * len(PARTS)


def split(v):
    hi = v.astype(BF16)
    return hi, (v - hi.astype(F32)).astype(BF16)


def dot3(ah, al, bh, bl, dims):
    def d(a, b):
        return lax.dot_general(a, b, dims, preferred_element_type=F32)

    return d(ah, bh) + d(ah, bl) + d(al, bh)


def evaluate(total, reach, own, par, out, xh, xl, sh, sl, nh, nl, rh, rl, between=None):
    gr, gc = lax.axis_index("gr"), lax.axis_index("gc")
    s = lax.rem(gc, 2)
    sg = 1 - 2 * s
    row = gr * 8 + gc
    at0 = 1 + 3 * s
    r = [reach[lax.rem(row + sg * (a - 8) + total, total)] for a in range(18)]

    def keep(a, b):
        ok = abs(a - b) <= jnp.minimum(r[a], r[b])
        return jnp.where(ok, 1.0, 0.0).astype(F32)

    def put(a, b, v):
        J, K = a // 2, b // 2
        rows = pl.ds((a % 2) * BS, BS)
        cols = pl.ds((K - J + 2) * G + (b % 2) * BS, BS)
        hi, lo = split(v)
        xh[J, rows, cols] = hi
        xl[J, rows, cols] = lo

    def both(a, b, v):
        if 0 <= b < 18:
            put(a, b, v)
            if a != b:
                put(b, a, v.T)

    zero = jnp.zeros((BS, BS), F32)

    def rows_here(k):
        a = 2 * k
        for d in range(-1, 5):
            if d == -1 and k == 0:
                continue
            both(a, a + d, own[k, at0 + sg * d])
        both(a, a - 3, own[k, 6])
        if a + 5 < 18:
            put(a, a + 5, zero)
            put(a + 5, a, zero)

    def all_here():
        for k in range(9):
            rows_here(k)

    if between is None:
        all_here()
    else:
        between(all_here)
    for k in range(9):
        for n in range(3):
            both(2 * k + 1, 2 * k + 1 + 2 * n, par[k, n])

    def span(J, lo, hi):
        return pl.ds((lo - J + 2) * G, (hi - lo + 1) * G)

    def masked(J, K, v):
        return jnp.concatenate(
            [
                jnp.concatenate([v[:BS, :BS] * keep(2 * J, 2 * K), v[:BS, BS:] * keep(2 * J, 2 * K + 1)], axis=1),
                jnp.concatenate([v[BS:, :BS] * keep(2 * J + 1, 2 * K), v[BS:, BS:] * keep(2 * J + 1, 2 * K + 1)], axis=1),
            ],
            axis=0,
        )

    for J in range(2, 7):
        for K in range(J - 2, J + 3):
            if 2 <= K < J:
                continue
            lo, hi = max(J, K) - 2, min(J, K) + 2
            a, b = span(J, lo, hi), span(K, lo, hi)
            v = masked(J, K, dot3(xh[J, :, a], xl[J, :, a], xh[K, :, b], xl[K, :, b], NT))
            cols = span(J, K, K)
            sh[J - 2, :, cols], sl[J - 2, :, cols] = split(v)
            if J < K < 7:
                cols = span(K, J, J)
                sh[K - 2, :, cols], sl[K - 2, :, cols] = split(v.T)
    for J in range(2, 7):
        for K in range(max(2, J - 2), min(6, J + 2) + 1):
            lo, hi = max(J, K) - 2, min(J, K) + 2
            a, b = span(J, lo, hi), span(K, lo, hi)
            cube = dot3(sh[J - 2, :, a], sl[J - 2, :, a], xh[K, :, b], xl[K, :, b], NT)
            cols = span(J, K, K)
            square = sh[J - 2, :, cols].astype(F32) + sl[J - 2, :, cols].astype(F32)
            hi_, lo_ = split(masked(J, K, 3.0 * square - 2.0 * cube))
            rows = span(K, J, J)
            nh[K - 2, rows, :] = hi_
            nl[K - 2, rows, :] = lo_
            if J == 4:
                rh[:, cols] = hi_[:BS]
                rl[:, cols] = lo_[:BS]
    squares = []
    for K in range(2, 7):
        lo, hi = max(4, K) - 2, min(4, K) + 2
        a, b = span(4, lo, hi), span(K, lo, hi)
        v = dot3(rh[:, a], rl[:, a], nh[K - 2, b, :], nl[K - 2, b, :], NN)
        v = jnp.concatenate([v[:, :BS] * keep(8, 2 * K), v[:, BS:] * keep(8, 2 * K + 1)], axis=1)
        squares.append(v)
    sq = [split(v) for v in squares]
    for K in range(2, 7):
        lo, hi = max(4, K) - 2, min(4, K) + 2
        b = span(K, lo, hi)
        ah = jnp.concatenate([sq[L - 2][0] for L in range(lo, hi + 1)], axis=1)
        al = jnp.concatenate([sq[L - 2][1] for L in range(lo, hi + 1)], axis=1)
        v = 3.0 * squares[K - 2] - 2.0 * dot3(ah, al, nh[K - 2, b, :], nl[K - 2, b, :], NN)
        for h in range(2):
            m = 2 * K + h
            if abs(m - 8) <= 4:
                out[0, 4 + sg * (m - 8)] = v[:, h * BS : (h + 1) * BS] * keep(8, m)


WORK = [
    pltpu.VMEM((9, G, 5 * G), BF16),
    pltpu.VMEM((9, G, 5 * G), BF16),
    pltpu.VMEM((5, G, 5 * G), BF16),
    pltpu.VMEM((5, G, 5 * G), BF16),
    pltpu.VMEM((5, 5 * G, G), BF16),
    pltpu.VMEM((5, 5 * G, G), BF16),
    pltpu.VMEM((BS, 5 * G), BF16),
    pltpu.VMEM((BS, 5 * G), BF16),
]
LAND = [(9, 7, BS, BS), (9, 3, BS, BS)]
SEMS = [pltpu.SemaphoreType.DMA((COPIES,)), pltpu.SemaphoreType.DMA((COPIES,)), pltpu.SemaphoreType.DMA((2,))]
VMEM_LIMIT = 58 << 20


def solution(mesh):
    lines = mesh.shape["gr"]
    spec = P(("gr", "gc"), None, None, None)

    def local(density, reach):
        total = reach.shape[0]

        def kernel(reach_ref, x_ref, out_ref, own, par, ssem, rsem, lsem, *work):
            def between(meanwhile):
                exchange(lines, x_ref, own, par, ssem, rsem, lsem, meanwhile)

            evaluate(total, reach_ref, own, par, out_ref, *work, between=between)

        return pl.pallas_call(
            kernel,
            out_shape=jax.ShapeDtypeStruct(density.shape, F32),
            in_specs=[pl.BlockSpec(memory_space=pltpu.SMEM), pl.BlockSpec(memory_space=pl.ANY)],
            out_specs=pl.BlockSpec(memory_space=pltpu.VMEM),
            scratch_shapes=[pltpu.VMEM(shape, F32) for shape in LAND] + SEMS + WORK,
            compiler_params=pltpu.CompilerParams(collective_id=0, has_side_effects=True, vmem_limit_bytes=VMEM_LIMIT),
        )(reach, density)

    return jax.shard_map(local, mesh=mesh, in_specs=(spec, P()), out_specs=spec, check_vma=False)
```

```python
import jax
import jax.numpy as jnp
from jax import lax
from jax.experimental import pallas as pl
from jax.experimental.pallas import tpu as pltpu
from jax.sharding import PartitionSpec as P

MESH = pl.DeviceIdType.MESH
BS = 128
G = 2 * BS
HB = BS // 2
F32 = jnp.float32
BF16 = jnp.bfloat16
NT = (((1,), (1,)), ((), ()))
NN = (((1,), (0,)), ((), ()))


def triangles():
    r = lax.broadcasted_iota(jnp.int32, (HB, HB), 0)
    c = lax.broadcasted_iota(jnp.int32, (HB, HB), 1)
    return r, c


def pack(v):
    r, c = triangles()
    low = v[HB:, HB:]
    both = jnp.where(r <= c, v[:HB, :HB], low)
    diagonal = jnp.sum(jnp.where(r == c, low, 0.0), axis=0, keepdims=True)
    tail = jnp.concatenate([diagonal, jnp.zeros((1, HB), F32)], axis=1)
    return jnp.concatenate([both, v[:HB, HB:]], axis=1), jnp.broadcast_to(tail, (8, BS))


def unpack(top, tail):
    r, c = triangles()
    both, corner = top[:, :HB], top[:, HB:]
    turned = both.T
    high = jnp.where(r <= c, both, turned)
    low = jnp.where(r > c, both, jnp.where(r < c, turned, jnp.broadcast_to(tail[:1, :HB], (HB, HB))))
    return jnp.concatenate(
        [jnp.concatenate([high, corner], axis=1), jnp.concatenate([corner.T, low], axis=1)], axis=0
    )


def exchange(lines, x_ref, own, par, packed, ssem, rsem, lsem, meanwhile=lambda: None):
    gr, gc = lax.axis_index("gr"), lax.axis_index("gc")
    x, s = gc // 2, lax.rem(gc, 2)
    sg = 1 - 2 * s
    side = 2 * lax.rem(gr, 2) - 1
    partner_gc = gc + sg
    partner = (gr, partner_gc)
    next_line = lax.rem(gr + side + lines, lines)
    out = (next_line, gc)
    mate = (gr - side, gc)
    steps = (1, 3, 2)
    others = [lax.rem(x + step, 4) for step in steps]
    peers = [(gr, o * 2 + s) for o in others]

    own_wide = pltpu.make_async_copy(x_ref.at[0, pl.ds(3 - 3 * s, 6)], own.at[4, pl.ds(0, 6)], lsem.at[0])
    own_far = pltpu.make_async_copy(x_ref.at[0, 4 - 3 * sg], own.at[4, 6], lsem.at[1])
    own_wide.start()
    own_far.start()

    barrier = pltpu.get_barrier_semaphore()
    pair, pairs = gr * 4 + x, lines * 4
    around, extra = [], 0
    for k in HOPS:
        q = pair + k
        wraps = jnp.logical_or(q < 0, q >= pairs)
        q = lax.rem(q + pairs, pairs)
        same = (q // 4, lax.rem(q, 4) * 2 + s)
        flipped = (same[0], same[1] + sg)
        around.append((k, wraps, same, flipped))
        extra = extra + jnp.where(wraps, 1, 0)
    for d in [partner] + [a[2] for a in around]:
        pl.semaphore_signal(barrier, inc=1, device_id=d, device_id_type=MESH)
    for _, wraps, _, flipped in around:

        @pl.when(wraps)
        def _(flipped=flipped):
            pl.semaphore_signal(barrier, inc=1, device_id=flipped, device_id_type=MESH)

    own_wide.wait()
    own_far.wait()
    packed[pl.ds(0, HB), :], packed[pl.ds(HB, 8), :] = pack(own[4, 1 + 3 * s])
    pl.semaphore_wait(barrier, 1 + len(HOPS) + extra)

    pending = []

    def copy(src, dst, device, k, arrives=None):
        c = pltpu.make_async_remote_copy(
            src, dst, ssem.at[k], rsem.at[k if arrives is None else arrives], device_id=device, device_id_type=MESH
        )
        pending.append(c)
        return c

    slot_out, slot_back = 4 + 4 * sg * side, 4 - 4 * sg * side

    def routes(buffer, base, pick):
        def at(slot):
            return pick(buffer, slot)

        here = at(4)
        near = [copy(here, at(slot_back), out, base), copy(here, at(slot_out), mate, base + 1)]
        line, onward = [], []
        for j, (step, o, dst) in enumerate(zip(steps, others, peers)):
            line.append(copy(here, at(4 + sg * (x - o)), dst, base + 2 + j, base + 2 + (1, 0, 2)[j]))
            to_peer = (o - x) * side > 0
            src = jnp.where(to_peer, slot_out, 4 + sg * (o - x))
            k = jnp.where(to_peer, x - o, o - x)
            dst_slot = 4 + sg * (k + 4 * side)
            device = (jnp.where(to_peer, dst[0], mate[0]), jnp.where(to_peer, dst[1], mate[1]))
            arrives = base + 5 + jnp.where(to_peer, (1, 0, 2)[j], j)
            onward.append((to_peer, copy(at(src), at(dst_slot), device, base + 5 + j, arrives)))
        return near, line, onward

    def arrived(j, base, piece):
        return pltpu.make_async_remote_copy(
            piece, piece, ssem.at[base + 5 + j], rsem.at[base + 5 + j], device_id=mate, device_id_type=MESH
        )

    def start_if(cond, c):
        @pl.when(cond)
        def _():
            c.start()

    early = [routes(own, 5 + 8 * e, lambda ref, slot, p=p: ref.at[slot, p]) for e, p in enumerate(PIECES)]
    base = 5 + 8 * len(PIECES)
    mine = [packed if n == 0 else x_ref.at[(0, 4 - 2 * q[0] * sg) + q[1:]] for n, q in enumerate(PARTS)]
    cross = [copy(mine[n], par.at[(4,) + q], partner, n) for n, q in enumerate(PARTS)]
    hot = (next_line // 8) != (gr // 8)

    for near, _, _ in early:
        near[0].start()
    for c in cross:
        c.start()
    late = []
    for n, q in enumerate(PARTS):
        copies = []
        for j, (k, wraps, same, flipped) in enumerate(around):
            sem, there = base + 8 * n + j, base + 8 * n + (j ^ 1)
            c = copy(par.at[(4,) + q], par.at[(4 - sg * k,) + q], same, sem, there)
            copies.append((wraps, c))
            own_row = pltpu.make_async_remote_copy(
                mine[n],
                par.at[(4 + sg * k,) + q],
                ssem.at[sem],
                rsem.at[there],
                device_id=flipped,
                device_id_type=MESH,
            )
            start_if(wraps, own_row)
        late.append(copies)
    for _, line, _ in early:
        for c in line:
            c.start()
    for near, _, _ in early:
        near[1].start()

    def pass_out(route):
        near, _, onward = route
        near[0].wait_recv()
        for to_peer, c in onward:
            start_if(to_peer, c)

    def pass_mate(route):
        _, line, onward = route
        for j, (to_peer, c) in enumerate(onward):
            line[(1, 0, 2)[j]].wait_recv()
            start_if(jnp.logical_not(to_peer), c)

    def spread(n):
        cross[n].wait_recv()
        for wraps, c in late[n]:
            start_if(jnp.logical_not(wraps), c)

    for route in early:
        pass_mate(route)
    spread(0)

    @pl.when(jnp.logical_not(hot))
    def _():
        for route in early:
            pass_out(route)

    for n in range(1, len(PARTS)):
        spread(n)

    @pl.when(hot)
    def _():
        for route in early:
            pass_out(route)

    for e, p in enumerate(PIECES):
        early[e][0][1].wait_recv()
        for j in range(3):
            arrived(j, 5 + 8 * e, own.at[4, p]).wait_recv()
    meanwhile()
    for copies in late:
        for _, c in copies:
            c.wait_recv()
    for c in pending:
        c.wait_send()


HOPS = (4, -4, 3, -3, 2, -2, 1, -1)
PIECES = (pl.ds(0, 7),)
PARTS = ((0, pl.ds(0, 72)), (1,), (2,))
COPIES = 5 + 8 * len(PIECES) + 8 * len(PARTS)


def split(v):
    hi = v.astype(BF16)
    return hi, (v - hi.astype(F32)).astype(BF16)


def dot3(ah, al, bh, bl, dims):
    def d(a, b):
        return lax.dot_general(a, b, dims, preferred_element_type=F32)

    return d(ah, bh) + d(ah, bl) + d(al, bh)


def evaluate(total, reach, own, par, out, xh, xl, sh, sl, nh, nl, rh, rl, between=None):
    gr, gc = lax.axis_index("gr"), lax.axis_index("gc")
    s = lax.rem(gc, 2)
    sg = 1 - 2 * s
    row = gr * 8 + gc
    at0 = 1 + 3 * s
    r = [reach[lax.rem(row + sg * (a - 8) + total, total)] for a in range(18)]

    def keep(a, b):
        ok = abs(a - b) <= jnp.minimum(r[a], r[b])
        return jnp.where(ok, 1.0, 0.0).astype(F32)

    def put(a, b, v):
        J, K = a // 2, b // 2
        rows = pl.ds((a % 2) * BS, BS)
        cols = pl.ds((K - J + 2) * G + (b % 2) * BS, BS)
        hi, lo = split(v)
        xh[J, rows, cols] = hi
        xl[J, rows, cols] = lo

    def both(a, b, v):
        if 0 <= b < 18:
            put(a, b, v)
            if a != b:
                put(b, a, v.T)

    zero = jnp.zeros((BS, BS), F32)

    def rows_here(k):
        a = 2 * k
        for d in range(-1, 5):
            if d == -1 and k == 0:
                continue
            both(a, a + d, own[k, at0 + sg * d])
        both(a, a - 3, own[k, 6])
        if a + 5 < 18:
            put(a, a + 5, zero)
            put(a + 5, a, zero)

    def all_here():
        for k in range(9):
            rows_here(k)

    if between is None:
        all_here()
    else:
        between(all_here)
    for k in range(9):
        put(2 * k + 1, 2 * k + 1, unpack(par[k, 0, pl.ds(0, HB), :], par[k, 0, pl.ds(HB, 8), :]))
        for n in (1, 2):
            both(2 * k + 1, 2 * k + 1 + 2 * n, par[k, n])

    def span(J, lo, hi):
        return pl.ds((lo - J + 2) * G, (hi - lo + 1) * G)

    def masked(J, K, v):
        return jnp.concatenate(
            [
                jnp.concatenate([v[:BS, :BS] * keep(2 * J, 2 * K), v[:BS, BS:] * keep(2 * J, 2 * K + 1)], axis=1),
                jnp.concatenate([v[BS:, :BS] * keep(2 * J + 1, 2 * K), v[BS:, BS:] * keep(2 * J + 1, 2 * K + 1)], axis=1),
            ],
            axis=0,
        )

    for J in range(2, 7):
        for K in range(J - 2, J + 3):
            if 2 <= K < J:
                continue
            lo, hi = max(J, K) - 2, min(J, K) + 2
            a, b = span(J, lo, hi), span(K, lo, hi)
            v = masked(J, K, dot3(xh[J, :, a], xl[J, :, a], xh[K, :, b], xl[K, :, b], NT))
            cols = span(J, K, K)
            sh[J - 2, :, cols], sl[J - 2, :, cols] = split(v)
            if J < K < 7:
                cols = span(K, J, J)
                sh[K - 2, :, cols], sl[K - 2, :, cols] = split(v.T)
    for J in range(2, 7):
        for K in range(max(2, J - 2), min(6, J + 2) + 1):
            lo, hi = max(J, K) - 2, min(J, K) + 2
            a, b = span(J, lo, hi), span(K, lo, hi)
            cube = dot3(sh[J - 2, :, a], sl[J - 2, :, a], xh[K, :, b], xl[K, :, b], NT)
            cols = span(J, K, K)
            square = sh[J - 2, :, cols].astype(F32) + sl[J - 2, :, cols].astype(F32)
            hi_, lo_ = split(masked(J, K, 3.0 * square - 2.0 * cube))
            rows = span(K, J, J)
            nh[K - 2, rows, :] = hi_
            nl[K - 2, rows, :] = lo_
            if J == 4:
                rh[:, cols] = hi_[:BS]
                rl[:, cols] = lo_[:BS]
    squares = []
    for K in range(2, 7):
        lo, hi = max(4, K) - 2, min(4, K) + 2
        a, b = span(4, lo, hi), span(K, lo, hi)
        v = dot3(rh[:, a], rl[:, a], nh[K - 2, b, :], nl[K - 2, b, :], NN)
        v = jnp.concatenate([v[:, :BS] * keep(8, 2 * K), v[:, BS:] * keep(8, 2 * K + 1)], axis=1)
        squares.append(v)
    sq = [split(v) for v in squares]
    for K in range(2, 7):
        lo, hi = max(4, K) - 2, min(4, K) + 2
        b = span(K, lo, hi)
        ah = jnp.concatenate([sq[L - 2][0] for L in range(lo, hi + 1)], axis=1)
        al = jnp.concatenate([sq[L - 2][1] for L in range(lo, hi + 1)], axis=1)
        v = 3.0 * squares[K - 2] - 2.0 * dot3(ah, al, nh[K - 2, b, :], nl[K - 2, b, :], NN)
        for h in range(2):
            m = 2 * K + h
            if abs(m - 8) <= 4:
                out[0, 4 + sg * (m - 8)] = v[:, h * BS : (h + 1) * BS] * keep(8, m)


WORK = [
    pltpu.VMEM((9, G, 5 * G), BF16),
    pltpu.VMEM((9, G, 5 * G), BF16),
    pltpu.VMEM((5, G, 5 * G), BF16),
    pltpu.VMEM((5, G, 5 * G), BF16),
    pltpu.VMEM((5, 5 * G, G), BF16),
    pltpu.VMEM((5, 5 * G, G), BF16),
    pltpu.VMEM((BS, 5 * G), BF16),
    pltpu.VMEM((BS, 5 * G), BF16),
]
LAND = [(9, 7, BS, BS), (9, 3, BS, BS)]
SEMS = [pltpu.SemaphoreType.DMA((COPIES,)), pltpu.SemaphoreType.DMA((COPIES,)), pltpu.SemaphoreType.DMA((2,))]
VMEM_LIMIT = 58 << 20


def solution(mesh):
    lines = mesh.shape["gr"]
    spec = P(("gr", "gc"), None, None, None)

    def local(density, reach):
        total = reach.shape[0]

        def kernel(reach_ref, x_ref, out_ref, own, par, packed, ssem, rsem, lsem, *work):
            def between(meanwhile):
                exchange(lines, x_ref, own, par, packed, ssem, rsem, lsem, meanwhile)

            evaluate(total, reach_ref, own, par, out_ref, *work, between=between)

        return pl.pallas_call(
            kernel,
            out_shape=jax.ShapeDtypeStruct(density.shape, F32),
            in_specs=[pl.BlockSpec(memory_space=pltpu.SMEM), pl.BlockSpec(memory_space=pl.ANY)],
            out_specs=pl.BlockSpec(memory_space=pltpu.VMEM),
            scratch_shapes=[pltpu.VMEM(shape, F32) for shape in LAND] + [pltpu.VMEM((72, BS), F32)] + SEMS + WORK,
            compiler_params=pltpu.CompilerParams(collective_id=0, has_side_effects=True, vmem_limit_bytes=VMEM_LIMIT),
        )(reach, density)

    return jax.shard_map(local, mesh=mesh, in_specs=(spec, P()), out_specs=spec, check_vma=False)
```
